512 devices in a mesh: basis: 2 (over z_hi), eig: 32 (over y, z_lo), chan: 8 (over x, core).
Axes of the slice: x: 4, y: 4, z: 16 (z_hi: 2, z_lo: 8; z = z_hi * 8 + z_lo), core: 2. Of those that a mesh axis runs over, the one named last changes fastest.
Arguments:
- eigvecs: bfloat16 [2048, 5120], P('eig', 'basis'), may hold values from -6 to 6
- boundary: bfloat16 [5120, 4096], P('basis', 'chan'), may hold values from -0.3125 to 0.3125
- block_sizes: int32 [16], replicated, may hold values from 256 to 768, as said below
- target_of_channel: int32 [4096], P('chan'), may hold values from 0 to 15, as said below
- poles: float32 [2048], replicated, may hold values from -4 to 4, as said below
- energies: float32 [16], P('basis'), may hold values from -0.25 to 0.25
Outputs:
- rmatrix: float32 [16, 4096, 4096], P('basis', 'chan', 'eig')
The draws below stay inside these ranges and needn't reach their ends.
Inputs may be any that keep to these rules, and one draw needn't show every extreme that they name: `poles`: every pole lies 0.5 or more away from zero, with both signs present. `block_sizes`: the sizes sum to 5120; every target state's block holds at least 256 basis rows. `target_of_channel`: every target state has exactly 256 channels.
All inputs are finite; a program needn't handle non-finite values.
Results may differ from the reference program's by a relative error of at most 0.0049.
Values may be sent and summed in bfloat16 or wider, within the bound.
A program may use at most 128 MiB of HBM per device.

```python
import jax
import jax.numpy as jnp
from jax import lax

C = 4096
NT = 16
K = 2048
NB = 5120
NE = 16
LEAST = 256
MOST = 768


def draw_poles(key, part):
    sign_key, size_key = jax.random.split(jax.random.fold_in(key, 11))
    signs = jnp.where(jax.random.randint(sign_key, (K,), 0, 2) == 1, 1.0, -1.0).astype(jnp.float32)
    sizes_drawn = jnp.exp(jax.random.uniform(size_key, (K,), jnp.float32, jnp.log(0.5), jnp.log(4.0)))
    return (signs * sizes_drawn).astype(jnp.float32)


def draw_block_sizes(key, part):
    cut_key, pick_key = jax.random.split(jax.random.fold_in(key, 23))
    half_share = MOST - LEAST
    rest_share = NB - C - half_share
    cuts = jnp.sort(jax.random.randint(cut_key, (NT - 2,), 0, rest_share + 1).astype(jnp.int32))
    edges = jnp.concatenate([jnp.zeros((1,), jnp.int32), cuts, jnp.full((1,), rest_share, jnp.int32)])
    others = edges[1:] - edges[:-1]
    special = jax.random.randint(pick_key, (), 0, NT).astype(jnp.int32)
    slots = jnp.arange(NT, dtype=jnp.int32)
    position = jnp.clip(slots - (slots > special).astype(jnp.int32), 0, NT - 2)
    shares = jnp.where(slots == special, half_share, others[position])
    return (LEAST + shares).astype(jnp.int32)


def draw_target_of_channel(key, part):
    order = jax.random.permutation(jax.random.fold_in(key, 37), C)
    return (order // LEAST).astype(jnp.int32)


def block_levels(key, extent, pieces, low, top_value):
    loudness = 1.0
    for dim, blocks in pieces:
        heights = jax.random.uniform(jax.random.fold_in(jax.random.fold_in(key, 6), dim), (blocks,), jnp.float32, low / len(pieces), top_value / len(pieces))
        loudness = loudness * jnp.repeat(jnp.exp(heights), extent[dim] // blocks).reshape((-1,) + (1,) * (len(extent) - 1 - dim))
    return loudness


def bell_draw(stream_key, extent, scale, most, shards=(), kind=jnp.bfloat16):
    values = jax.random.normal(stream_key, extent, jnp.float32) * scale
    if len(shards) > 0:
        values = block_levels(stream_key, extent, shards, -0.22, 0.18) * values
    return jnp.clip(values, min=-most, max=most).astype(kind)


def setup_inputs(seed: int = 0) -> dict:
    streams_of = jax.random.split(jax.random.key(seed), 7)
    eigvecs = bell_draw(streams_of[0], (K, NB), 1.0, 6.0, ((0, 32), (1, 2)))
    boundary = bell_draw(streams_of[1], (NB, C), (NB // NT) ** -0.5, 0.3125, ((0, 2), (1, 8)))
    block_sizes = draw_block_sizes(jax.random.fold_in(streams_of[6], 71), 0)
    target_of_channel = draw_target_of_channel(jax.random.fold_in(streams_of[6], 71), 0)
    poles = draw_poles(jax.random.fold_in(streams_of[6], 71), 0)
    energies = jnp.clip(jax.random.uniform(streams_of[5], (NE,), jnp.float32, -0.25, 0.25) * block_levels(streams_of[5], (NE,), ((0, 2),), -0.4, 0.0), -0.25, 0.25)
    return dict(eigvecs=eigvecs, boundary=boundary, block_sizes=block_sizes, target_of_channel=target_of_channel, poles=poles, energies=energies)


def reference(eigvecs, boundary, block_sizes, target_of_channel, poles, energies):
    block_ends = jnp.cumsum(block_sizes).astype(jnp.int32)
    row_ids = jnp.arange(NB, dtype=jnp.int32)
    owner_of = jnp.sum((block_ends[None, :] <= row_ids[:, None]).astype(jnp.int32), axis=1).astype(jnp.int32)
    member = owner_of[:, None] == target_of_channel[None, :]
    masked = jnp.where(member, boundary, jnp.zeros_like(boundary))
    amplitudes = jnp.dot(eigvecs, masked, preferred_element_type=jnp.float32).astype(jnp.bfloat16)
    weights = 1.0 / (poles[None, :] - energies[:, None])
    factor = K ** -0.5

    def per_energy(weight_row):
        scaled = (weight_row[:, None] * amplitudes.astype(jnp.float32)).astype(jnp.bfloat16)
        return jnp.dot(scaled.T, amplitudes, preferred_element_type=jnp.float32) * factor

    return lax.map(per_energy, weights)
```

```python
import jax
import jax.numpy as jnp
from jax import lax
from jax.experimental import pallas as pl
from jax.experimental.pallas import tpu as pltpu
from jax.sharding import PartitionSpec as P

MESH = pl.DeviceIdType.MESH
NY, NZL, NX = 4, 8, 4
NS = 2


def remote(src, dst, send, recv, where):
    return pltpu.make_async_remote_copy(
        src_ref=src, dst_ref=dst, send_sem=send, recv_sem=recv, device_id=where, device_id_type=MESH
    )


def kernel(
    eig_hbm, bnd_hbm, sizes, tgt, poles, energies, out,
    eig, bnd, part, psend, precv, G, D, wrow, wcol, LT, BS,
    eig_sem, bnd_sem, xs, xr, zs, zr, ys, yr, fs, fr, ds, dr,
):
    h, e, c = lax.axis_index("basis"), lax.axis_index("eig"), lax.axis_index("chan")
    y, zl = e // NZL, e % NZL
    x, core = c // 2, c % 2
    z = h * NZL + zl
    rows = bnd.shape[1]

    def at_z(zz):
        return (zz // NZL, y * NZL + zz % NZL, c)

    across = (1 - h, e, c)
    zplus, zminus = at_z((z + 1) % 16), at_z((z + 15) % 16)
    yplus = (h, ((y + 1) % NY) * NZL + zl, c)
    yminus = (h, ((y + 3) % NY) * NZL + zl, c)
    xplus = (h, e, ((x + 1) % NX) * 2 + core)
    xminus = (h, e, ((x + 3) % NX) * 2 + core)
    twin = (h, e, x * 2 + (1 - core))

    barrier = pltpu.get_barrier_semaphore()
    for who in (across, zplus, zminus, yplus, yminus, xplus, xminus, twin):
        pl.semaphore_signal(barrier, inc=1, device_id=who, device_id_type=MESH)

    eig_copy = pltpu.make_async_copy(eig_hbm, eig, eig_sem)
    eig_copy.start()

    def bnd_copy(b):
        return pltpu.make_async_copy(
            bnd_hbm.at[:, pl.ds(pl.multiple_of(b * 128, 128), 128)], bnd.at[b], bnd_sem.at[b]
        )

    for b in range(4):
        bnd_copy(b).start()
    eig_copy.wait()

    @pl.loop(0, 4)
    def _(b):
        bnd_copy(b).wait()
        t = tgt[pl.ds(b, 1), :]
        lo = jnp.zeros((1, 128), jnp.int32)
        hi = jnp.zeros((1, 128), jnp.int32)
        for k in range(16):
            lo = lo + jnp.where(t > k, sizes[k], 0)
            hi = hi + jnp.where(t >= k, sizes[k], 0)
        lo = lo - h * rows
        hi = hi - h * rows
        step = rows // 5
        total = jnp.zeros((64, 128), jnp.float32)
        for i in range(5):
            row = lax.broadcasted_iota(jnp.int32, (step, 128), 0) + i * step
            keep = jnp.logical_and(row >= lo, row < hi)
            vals = bnd[b, i * step : (i + 1) * step, :].astype(jnp.float32)
            masked = jnp.where(keep, vals, 0.0).astype(jnp.bfloat16)
            total = total + jnp.dot(
                eig[:, i * step : (i + 1) * step], masked, preferred_element_type=jnp.float32
            )
        part[b] = total
        psend[b] = total.astype(jnp.bfloat16)

    pl.semaphore_wait(barrier, 8)

    def cross(b):
        return remote(psend.at[b], precv.at[b], xs.at[b], xr.at[b], across)

    for b in range(4):
        cross(b).start()

    for k in range(8):
        wrow[k] = (wrow.shape[1] * 128) ** -0.5 / (poles[...] - energies[k])
    for i in range(16):
        turned = jnp.transpose(wrow[:, i, :])
        wcol[i // 4, (i % 4) * 2 : (i % 4) * 2 + 2] = turned.reshape(2, 64, 8)

    @pl.loop(0, 8)
    def _(k):
        out[k] = jnp.zeros(out.shape[1:], jnp.float32)

    def at(q):
        return (zl + ((q + 1) // 2) * (1 - 2 * (q % 2)) + NZL) % NZL

    def shard(s, yy, q):
        return G.at[pl.ds(s * (4 // NS), 4 // NS), yy, at(q)]

    def z_copy(s, up, q, nxt):
        return remote(
            shard(s, y, q), shard(s, y, q), zs.at[s, up, q], zr.at[s, nxt], zplus if up else zminus
        )

    def y_copy(s, up, q):
        return remote(
            shard(s, y, q), shard(s, y, q), ys.at[s, up, q], yr.at[s, up, q], yplus if up else yminus
        )

    def f_copy(s, up, q):
        yy = (y + (3 if up else 1)) % NY
        return remote(shard(s, yy, q), shard(s, yy, q), fs.at[s, q], fr.at[s, q], yplus if up else yminus)

    def d_copy(k, q):
        to = (twin, xplus, xminus)[k]
        return remote(D.at[:, at(q)], D.at[:, at(q)], ds.at[k, q], dr.at[q], to)

    kap = zl // 4
    r = (x - y + NX) % NX
    mine = core == kap
    origin = jnp.logical_and(mine, r == 0)

    def d_local(q):
        return pltpu.make_async_copy(G.at[zl % 4, :, at(q)], D.at[:, at(q)], dr.at[q])

    def sends_up(q):
        return jnp.logical_and(mine, jnp.logical_or(r == 0, jnp.logical_and(r == 1, q % 2 == 0)))

    def sends_down(q):
        return jnp.logical_and(mine, jnp.logical_or(r == 0, jnp.logical_and(r == 3, q % 2 == 1)))

    def z_up_from(q):
        return jnp.logical_or(q == 0, jnp.logical_and(q % 2 == 1, q + 2 < 8 - core))

    def z_down_from(q):
        return jnp.logical_and(q % 2 == 0, q + 2 < 8 + core)

    def do_z(s, q):
        @pl.when(q > 0)
        def _():
            z_copy(s, 1, q, q).wait_recv()

        @pl.when(z_up_from(q))
        def _():
            z_copy(s, 1, q, q + 1 + (q + 7) // 8).start()

        @pl.when(z_down_from(q))
        def _():
            z_copy(s, 0, q, q + 2 - q // 6).start()

    def do_y(s, q):
        y_copy(s, 1, q).start()
        y_copy(s, 0, q).start()

    def do_f(s, q):
        y_copy(s, 1, q).wait_recv()
        y_copy(s, 0, q).wait_recv()

        @pl.when(core == 0)
        def _():
            f_copy(s, 1, q).start()

        @pl.when(core == 1)
        def _():
            f_copy(s, 0, q).start()

    def do_d0(q):
        for s in range(NS):
            f_copy(s, 1, q).wait_recv()

        @pl.when(origin)
        def _():
            d_local(q).start()

    def do_d1(q):
        @pl.when(origin)
        def _():
            d_local(q).wait()

        @pl.when(jnp.logical_not(origin))
        def _():
            d_copy(0, q).wait_recv()

        @pl.when(mine)
        def _():
            d_copy(0, q).start()

        @pl.when(sends_up(q))
        def _():
            d_copy(1, q).start()

        @pl.when(sends_down(q))
        def _():
            d_copy(2, q).start()

    def do_mm(q):
        p = at(q)
        for b in range(4):
            LT[b * 128 : (b + 1) * 128, :] = jnp.transpose(G[b, :, p].reshape(256, 128))
        dv = D[:, p].reshape(256, 128).astype(jnp.float32)
        w = wcol[:, p].reshape(256, 8)
        for k in range(8):
            BS[k // 2, :, (k % 2) * 128 : (k % 2 + 1) * 128] = (w[:, k : k + 1] * dv).astype(jnp.bfloat16)

        @pl.loop(0, 4)
        def _(n):
            got = jnp.dot(LT[...], BS[n], preferred_element_type=jnp.float32)
            out[2 * n] += got[:, :128]
            out[2 * n + 1] += got[:, 128:]

    for b in range(4):
        cross(b).wait_recv()
        G[b, y, zl] = (part[b] + precv[b].astype(jnp.float32)).astype(jnp.bfloat16)

    LAG = 5

    @pl.loop(0, 8 + LAG)
    def _(q):
        @pl.when(q < 8)
        def _():
            for s in range(NS):
                do_z(s, q)
                do_y(s, q)

        @pl.when(jnp.logical_and(q >= 1, q < 9))
        def _():
            for s in range(NS):
                do_f(s, q - 1)

        @pl.when(jnp.logical_and(q >= 2, q < 10))
        def _():
            do_d0(q - 2)

        @pl.when(jnp.logical_and(q >= 3, q < 11))
        def _():
            do_d1(q - 3)

        @pl.when(q >= LAG)
        def _():
            do_mm(q - LAG)

    for b in range(4):
        cross(b).wait_send()

    @pl.loop(0, 8)
    def _(q):
        for s in range(NS):
            @pl.when(z_up_from(q))
            def _():
                z_copy(s, 1, q, q).wait_send()

            @pl.when(z_down_from(q))
            def _():
                z_copy(s, 0, q, q).wait_send()

            y_copy(s, 1, q).wait_send()
            y_copy(s, 0, q).wait_send()
            f_copy(s, 1, q).wait_send()

        @pl.when(mine)
        def _():
            d_copy(0, q).wait_send()

        @pl.when(sends_up(q))
        def _():
            d_copy(1, q).wait_send()

        @pl.when(sends_down(q))
        def _():
            d_copy(2, q).wait_send()


def per_device(eigvecs, boundary, block_sizes, target_of_channel, poles, energies):
    rows = boundary.shape[0]
    vm, sm, anyw = (
        pl.BlockSpec(memory_space=pltpu.VMEM), pl.BlockSpec(memory_space=pltpu.SMEM), pl.BlockSpec(memory_space=pl.ANY)
    )
    bf, f32, dma = jnp.bfloat16, jnp.float32, pltpu.SemaphoreType.DMA
    return pl.pallas_call(
        kernel,
        out_shape=jax.ShapeDtypeStruct((8, 512, 128), f32),
        in_specs=[anyw, anyw, sm, vm, vm, sm],
        out_specs=vm,
        scratch_shapes=[
            pltpu.VMEM((64, rows), bf),
            pltpu.VMEM((4, rows, 128), bf),
            pltpu.VMEM((4, 64, 128), f32),
            pltpu.VMEM((4, 64, 128), bf),
            pltpu.VMEM((4, 64, 128), bf),
            pltpu.VMEM((4, NY, NZL, 64, 128), bf),
            pltpu.VMEM((NY, NZL, 64, 128), bf),
            pltpu.VMEM((8, 16, 128), f32),
            pltpu.VMEM((NY, NZL, 64, 8), f32),
            pltpu.VMEM((512, 256), bf),
            pltpu.VMEM((4, 256, 256), bf),
            dma, dma((4,)), dma((4,)), dma((4,)),
            dma((NS, 2, 8)), dma((NS, 8)),
            dma((NS, 2, 8)), dma((NS, 2, 8)),
            dma((NS, 8)), dma((NS, 8)),
            dma((3, 8)), dma((8,)),
        ],
        compiler_params=pltpu.CompilerParams(
            collective_id=0, has_side_effects=True, vmem_limit_bytes=40 * 2**20
        ),
        cost_estimate=pl.CostEstimate(flops=2_400_000_000, bytes_accessed=5_000_000, transcendentals=0),
    )(eigvecs, boundary, block_sizes, target_of_channel.reshape(4, 128), poles.reshape(16, 128), energies)


def solution(mesh):
    placed = (P("eig", "basis"), P("basis", "chan"), P(), P("chan"), P(), P("basis"))
    return jax.shard_map(
        per_device, mesh=mesh, in_specs=placed, out_specs=P("basis", "chan", "eig"), check_vma=False
    )
```

```python
import jax
import jax.numpy as jnp
from jax import lax
from jax.experimental import pallas as pl
from jax.experimental.pallas import tpu as pltpu
from jax.sharding import PartitionSpec as P

MESH = pl.DeviceIdType.MESH
NY, NZL, NX, NZ = 4, 8, 4, 16
NS = 2
LAGS = (3, 6, 10, 12, 20)


def remote(src, dst, send, recv, where):
    return pltpu.make_async_remote_copy(
        src_ref=src, dst_ref=dst, send_sem=send, recv_sem=recv, device_id=where, device_id_type=MESH
    )


def kernel(
    eig_hbm, bnd_hbm, sizes_hbm, tgt_hbm, poles_hbm, energies_hbm, out,
    sizes, tgt, poles, energies, small_sem, eig, bnd, psend, precv, G, D, wrow, wcol, LT, BS,
    eig_sem, bnd_sem, xs, xr, zs, zf, zr, ys, yr, fs, fr, ds, dr,
):
    h, e, c = lax.axis_index("basis"), lax.axis_index("eig"), lax.axis_index("chan")
    y, zl = e // NZL, e % NZL
    x, core = c // 2, c % 2
    z = h * NZL + zl
    rows = bnd.shape[1]

    def at_z(far):
        zz = (z + far + NZ) % NZ
        return (zz // NZL, y * NZL + zz % NZL, c)

    y_to = [(h, ((y + k) % NY) * NZL + zl, c) for k in (1, 3)]
    x_to = [(h, e, ((x + k) % NX) * 2 + core) for k in (1, 3, 2)]
    twin = (h, e, x * 2 + (1 - core))
    partners = [at_z(k) for k in (4, -4, 1, -1, 2, -2)] + y_to + x_to + [twin]

    barrier = pltpu.get_barrier_semaphore()
    for who in partners:
        pl.semaphore_signal(barrier, inc=1, device_id=who, device_id_type=MESH)

    small = [
        pltpu.make_async_copy(src, dst, small_sem.at[i])
        for i, (src, dst) in enumerate(
            ((sizes_hbm, sizes), (tgt_hbm, tgt), (poles_hbm, poles), (energies_hbm, energies))
        )
    ]
    eig_copy = pltpu.make_async_copy(eig_hbm, eig, eig_sem)

    def bnd_copy(s):
        return pltpu.make_async_copy(bnd_hbm.at[:, s * 256 : (s + 1) * 256], bnd.at[s], bnd_sem.at[s])

    for copy in small:
        copy.start()
    eig_copy.start()
    for s in range(NS):
        bnd_copy(s).start()
    for copy in small:
        copy.wait()
    eig_copy.wait()

    def cross(s):
        down = (s - h) * (s - h)
        return remote(psend.at[s], precv.at[down], xs.at[s], xr.at[down], at_z(4 - 8 * down))

    step = rows // 5
    for s in range(NS):
        bnd_copy(s).wait()
        t = jnp.concatenate([tgt[2 * s : 2 * s + 1, :], tgt[2 * s + 1 : 2 * s + 2, :]], axis=1)
        lo = jnp.zeros((1, 256), jnp.int32)
        hi = jnp.zeros((1, 256), jnp.int32)
        for k in range(16):
            lo = lo + jnp.where(t > k, sizes[k], 0)
            hi = hi + jnp.where(t >= k, sizes[k], 0)
        lo = lo - h * rows
        hi = hi - h * rows
        total = jnp.zeros((64, 256), jnp.float32)
        for i in range(5):
            row = lax.broadcasted_iota(jnp.int32, (step, 256), 0) + i * step
            keep = jnp.logical_and(row >= lo, row < hi)
            vals = bnd[s, i * step : (i + 1) * step, :].astype(jnp.float32)
            masked = jnp.where(keep, vals, 0.0).astype(jnp.bfloat16)
            total = total + jnp.dot(
                eig[:, i * step : (i + 1) * step], masked, preferred_element_type=jnp.float32
            )
        for j in range(2):
            psend[s, j] = total[:, j * 128 : (j + 1) * 128].astype(jnp.bfloat16)
        if s == 0:
            pl.semaphore_wait(barrier, len(partners))
        cross(s).start()

    for k in range(8):
        wrow[k] = (wrow.shape[1] * 128) ** -0.5 / (poles[...] - energies[k])
    for i in range(16):
        turned = jnp.transpose(wrow[:, i, :])
        wcol[i // 4, (i % 4) * 2 : (i % 4) * 2 + 2] = turned.reshape(2, 64, 8)

    @pl.loop(0, 8)
    def _(k):
        out[k] = jnp.zeros(out.shape[1:], jnp.float32)

    def shard(q, yy):
        m = (z + ((q + 1) // 2) * (1 - 2 * (q % 2)) + NZ) % NZ
        return G.at[((m + 12) % NZ) // NZL, :, yy, (m + 4) % NZL]

    def z_own(k):
        far, q = ((2, 3), (-2, 4), (1, 1), (-1, 2))[k]
        return remote(shard(0, y), shard(0, y), zs.at[k], zr.at[q], at_z(far))

    def z_up(q):
        return remote(shard(q, y), shard(q, y), zf.at[q], zr.at[q + 4], at_z(2))

    def z_down(q):
        return remote(shard(q, y), shard(q, y), zf.at[q], zr.at[q + 4 - q // 12], at_z(-2))

    def goes_up(q):
        return jnp.logical_and(q % 2 == 1, q + core < 12)

    def goes_down(q):
        return jnp.logical_and(jnp.logical_and(q % 2 == 0, q > 0), q < 12 + core)

    def y_copy(k, q):
        return remote(shard(q, y), shard(q, y), ys.at[k, q], yr.at[k, q], y_to[k])

    def f_copy(q):
        yy = (y + 3 - 2 * core) % NY
        to = (h, ((y + 1 + 2 * core) % NY) * NZL + zl, c)
        return remote(shard(q, yy), shard(q, yy), fs.at[q], fr.at[q], to)

    def at(q):
        return (zl + ((q + 1) // 2) * (1 - 2 * (q % 2)) + 20) % NZL

    def needed(q):
        m = (z + ((q + 1) // 2) * (1 - 2 * (q % 2)) + NZ) % NZ
        return ((m + 12) % NZ) // NZL == (zl % 4) // 2

    kap = zl // 4
    r = (x - y + NX) % NX
    mine = core == kap
    origin = jnp.logical_and(mine, r == 0)
    relay = jnp.logical_and(mine, r != 0)

    def d_copy(k, q):
        p = at(q)
        return remote(G.at[(zl % 4) // 2, zl % 2, :, p], D.at[:, p], ds.at[k, q], dr.at[q], (x_to + [twin])[k])

    def d_twin(q):
        p = at(q)
        return remote(D.at[:, p], D.at[:, p], ds.at[3, q], dr.at[q], twin)

    def d_local(q):
        p = at(q)
        return pltpu.make_async_copy(G.at[(zl % 4) // 2, zl % 2, :, p], D.at[:, p], dr.at[q])

    cross(0).wait_recv()
    cross(1).wait_recv()
    for j in range(2):
        both = precv[0, j].astype(jnp.float32) + precv[1, j].astype(jnp.float32)
        G[((z + 12) % NZ) // NZL, j, y, (zl + 4) % NZL] = both.astype(jnp.bfloat16)
    for k in range(4):
        z_own(k).start()

    def do_z(q):
        @pl.when(q > 0)
        def _():
            remote(shard(q, y), shard(q, y), zf.at[q], zr.at[q], at_z(1)).wait_recv()

        @pl.when(goes_up(q))
        def _():
            z_up(q).start()

        @pl.when(goes_down(q))
        def _():
            z_down(q).start()

        for k in range(2):
            y_copy(k, q).start()

    def do_f(q):
        for k in range(2):
            y_copy(k, q).wait_recv()
        f_copy(q).start()

    def do_d0(q):
        f_copy(q).wait_recv()

        @pl.when(jnp.logical_and(origin, needed(q)))
        def _():
            for k in (2, 0, 1, 3):
                d_copy(k, q).start()
            d_local(q).start()

    def do_d1(q):
        @pl.when(jnp.logical_and(origin, needed(q)))
        def _():
            d_local(q).wait()

        @pl.when(jnp.logical_and(relay, needed(q)))
        def _():
            d_twin(q).wait_recv()
            d_twin(q).start()

    def do_d2(q):
        @pl.when(jnp.logical_and(jnp.logical_not(mine), needed(q)))
        def _():
            d_twin(q).wait_recv()

    def do_mm(i):
        p = (zl + 12 + ((8 - i) // 2) * (2 * (i % 2) - 1)) % NZL
        for b in range(4):
            LT[b * 128 : (b + 1) * 128, :] = jnp.transpose(G[b // 2, b % 2, :, p].reshape(256, 128))
        dv = D[:, p].reshape(256, 128).astype(jnp.float32)
        w = wcol[:, p].reshape(256, 8)
        for k in range(8):
            BS[k // 2, :, (k % 2) * 128 : (k % 2 + 1) * 128] = (w[:, k : k + 1] * dv).astype(jnp.bfloat16)

        @pl.loop(0, 4)
        def _(n):
            got = jnp.dot(LT[...], BS[n], preferred_element_type=jnp.float32)
            out[2 * n] += got[:, :128]
            out[2 * n + 1] += got[:, 128:]

    def during(t, lag, count, do):
        @pl.when(jnp.logical_and(t >= lag, t < lag + count))
        def _():
            do(t - lag)

    @pl.loop(0, LAGS[-1] + 8)
    def _(t):
        during(t, 0, 16, do_z)
        during(t, LAGS[0], 16, do_f)
        during(t, LAGS[1], 16, do_d0)
        during(t, LAGS[2], 16, do_d1)
        during(t, LAGS[3], 16, do_d2)
        during(t, LAGS[4], 8, do_mm)

    for s in range(NS):
        cross(s).wait_send()
    for k in range(4):
        z_own(k).wait_send()

    @pl.loop(0, 16)
    def _(q):
        @pl.when(jnp.logical_or(goes_up(q), goes_down(q)))
        def _():
            z_up(q).wait_send()

        for k in range(2):
            y_copy(k, q).wait_send()
        f_copy(q).wait_send()

        @pl.when(jnp.logical_and(origin, needed(q)))
        def _():
            for k in range(4):
                d_copy(k, q).wait_send()

        @pl.when(jnp.logical_and(relay, needed(q)))
        def _():
            d_twin(q).wait_send()


def per_device(eigvecs, boundary, block_sizes, target_of_channel, poles, energies):
    rows = boundary.shape[0]
    bf, f32, dma = jnp.bfloat16, jnp.float32, pltpu.SemaphoreType.DMA
    given = (eigvecs, boundary, block_sizes, target_of_channel.reshape(4, 128), poles.reshape(16, 128), energies)
    return pl.pallas_call(
        kernel,
        out_shape=jax.ShapeDtypeStruct((8, 512, 128), f32),
        in_specs=[pl.BlockSpec(memory_space=pl.ANY)] * 6,
        out_specs=pl.BlockSpec(memory_space=pltpu.VMEM),
        scratch_shapes=[
            pltpu.SMEM((16,), jnp.int32),
            pltpu.VMEM((4, 128), jnp.int32),
            pltpu.VMEM((16, 128), f32),
            pltpu.SMEM((8,), f32),
            dma((4,)),
            pltpu.VMEM((64, rows), bf),
            pltpu.VMEM((NS, rows, 256), bf),
            pltpu.VMEM((2, 2, 64, 128), bf),
            pltpu.VMEM((2, 2, 64, 128), bf),
            pltpu.VMEM((2, 2, NY, NZL, 64, 128), bf),
            pltpu.VMEM((NY, NZL, 64, 128), bf),
            pltpu.VMEM((8, 16, 128), f32),
            pltpu.VMEM((NY, NZL, 64, 8), f32),
            pltpu.VMEM((512, 256), bf),
            pltpu.VMEM((4, 256, 256), bf),
            dma, dma((NS,)), dma((NS,)), dma((NS,)),
            dma((4,)), dma((16,)), dma((16,)),
            dma((2, 16)), dma((2, 16)),
            dma((16,)), dma((16,)),
            dma((4, 16)), dma((16,)),
        ],
        compiler_params=pltpu.CompilerParams(
            collective_id=0, has_side_effects=True, vmem_limit_bytes=42 * 2**20
        ),
        cost_estimate=pl.CostEstimate(flops=2_400_000_000, bytes_accessed=5_000_000, transcendentals=0),
    )(*(pltpu.with_memory_space_constraint(a, pltpu.HBM) for a in given))


def solution(mesh):
    placed = (P("eig", "basis"), P("basis", "chan"), P(), P("chan"), P(), P("basis"))
    return jax.shard_map(
        per_device, mesh=mesh, in_specs=placed, out_specs=P("basis", "chan", "eig"), check_vma=False
    )
```

```python
import jax
import jax.numpy as jnp
from jax import lax
from jax.experimental import pallas as pl
from jax.experimental.pallas import tpu as pltpu
from jax.sharding import PartitionSpec as P

MESH = pl.DeviceIdType.MESH
NY, NZL, NX, NZ = 4, 8, 4, 16
NS = 2
LAGS = (3, 5, 8, 9, 9)


def remote(src, dst, send, recv, where):
    return pltpu.make_async_remote_copy(
        src_ref=src, dst_ref=dst, send_sem=send, recv_sem=recv, device_id=where, device_id_type=MESH
    )


def kernel(
    eig_hbm, bnd_hbm, sizes_hbm, tgt_hbm, poles_hbm, energies_hbm, out,
    sizes, tgt, poles, energies, small_sem, eig, bnd, psend, precv, G, D, wrow, wcol, wide, LT, BS,
    eig_sem, bnd_sem, xs, xr, zs, zf, zr, ys, yr, fs, fr, ds, dr,
):
    h, e, c = lax.axis_index("basis"), lax.axis_index("eig"), lax.axis_index("chan")
    y, zl = e // NZL, e % NZL
    x, core = c // 2, c % 2
    z = h * NZL + zl
    rows = bnd.shape[0]

    def at_z(far):
        zz = (z + far + NZ) % NZ
        return (zz // NZL, y * NZL + zz % NZL, c)

    y_to = [(h, ((y + k) % NY) * NZL + zl, c) for k in (1, 3)]
    x_to = [(h, e, ((x + k) % NX) * 2 + core) for k in (1, 3, 2)]
    twin = (h, e, x * 2 + (1 - core))
    partners = [at_z(k) for k in (4, -4, 1, -1, 2, -2)] + y_to + x_to + [twin]

    barrier = pltpu.get_barrier_semaphore()
    for who in partners:
        pl.semaphore_signal(barrier, inc=1, device_id=who, device_id_type=MESH)

    small = [
        pltpu.make_async_copy(src, dst, small_sem.at[i])
        for i, (src, dst) in enumerate(
            ((sizes_hbm, sizes), (tgt_hbm, tgt), (poles_hbm, poles), (energies_hbm, energies))
        )
    ]
    eig_copy = pltpu.make_async_copy(eig_hbm, eig, eig_sem)

    step = rows // 5

    def bnd_copy(i):
        part = pl.ds(i * step, step)
        return pltpu.make_async_copy(bnd_hbm.at[part], bnd.at[part], bnd_sem.at[i])

    for copy in small:
        copy.start()
    eig_copy.start()
    for i in range(5):
        bnd_copy(i).start()
    for copy in small:
        copy.wait()

    def cross(s, down):
        return remote(psend.at[s], precv.at[down, s], xs.at[s, down], xr.at[s, down], at_z(4 - 8 * down))

    t = jnp.concatenate([tgt[b : b + 1, :] for b in range(4)], axis=1)
    lo = jnp.zeros((1, 512), jnp.int32)
    hi = jnp.zeros((1, 512), jnp.int32)
    for k in range(16):
        lo = lo + jnp.where(t > k, sizes[k], 0)
        hi = hi + jnp.where(t >= k, sizes[k], 0)
    lo = lo - h * rows
    hi = hi - h * rows
    eig_copy.wait()
    total = jnp.zeros((64, 512), jnp.float32)
    for i in range(5):
        bnd_copy(i).wait()
        row = lax.broadcasted_iota(jnp.int32, (step, 512), 0) + i * step
        keep = jnp.logical_and(row >= lo, row < hi)
        vals = bnd[i * step : (i + 1) * step, :].astype(jnp.float32)
        masked = jnp.where(keep, vals, 0.0).astype(jnp.bfloat16)
        total = total + jnp.dot(
            eig[:, i * step : (i + 1) * step], masked, preferred_element_type=jnp.float32
        )
    for b in range(4):
        psend[b // 2, b % 2] = total[:, b * 128 : (b + 1) * 128].astype(jnp.bfloat16)
    pl.semaphore_wait(barrier, len(partners))
    for s in range(NS):
        for down in range(2):
            cross(s, down).start()

    for k in range(8):
        wrow[k] = (wrow.shape[1] * 128) ** -0.5 / (poles[...] - energies[k])
    for i in range(16):
        wcol[i] = jnp.transpose(wrow[:, i, :])

    @pl.loop(0, 16)
    def _(i):
        for k in range(8):
            across = jnp.broadcast_to(wcol[i, :, k : k + 1], (128, 128))
            wide[k, i // 4, pl.ds((i % 4) * 2, 2)] = across.reshape(2, 64, 128)

    @pl.loop(0, 8)
    def _(k):
        out[k] = jnp.zeros(out.shape[1:], jnp.float32)

    def at(q):
        return (zl + ((q + 1) // 2) * (1 - 2 * (q % 2)) + 12) % NZL

    def shard(s, q, yy):
        return G.at[s, :, yy, at(q)]

    def z_own(s, k):
        far, q = ((2, 3), (-2, 4), (1, 1), (-1, 2))[k]
        return remote(shard(s, 0, y), shard(s, 0, y), zs.at[s, k], zr.at[s, q], at_z(far))

    def z_up(s, q):
        return remote(shard(s, q, y), shard(s, q, y), zf.at[s, q], zr.at[s, q + 4], at_z(2))

    def z_down(s, q):
        return remote(shard(s, q, y), shard(s, q, y), zf.at[s, q], zr.at[s, q + 4 - q // 4], at_z(-2))

    def goes_up(q):
        return jnp.logical_and(q % 2 == 1, q + core < 4)

    def goes_down(q):
        return jnp.logical_and(jnp.logical_and(q % 2 == 0, q > 0), q < 4 + core)

    def y_copy(s, k, q):
        return remote(shard(s, q, y), shard(s, q, y), ys.at[s, k, q], yr.at[s, k, q], y_to[k])

    def f_copy(s, q):
        yy = (y + 3 - 2 * core) % NY
        to = (h, ((y + 1 + 2 * core) % NY) * NZL + zl, c)
        return remote(shard(s, q, yy), shard(s, q, yy), fs.at[s, q], fr.at[s, q], to)

    kap = zl // 4
    r = (x - y + NX) % NX
    mine = core == kap
    origin = jnp.logical_and(mine, r == 0)
    relay = jnp.logical_and(mine, r != 0)

    def d_copy(k, q):
        p = at(q)
        return remote(G.at[(zl % 4) // 2, zl % 2, :, p], D.at[:, p], ds.at[k, q], dr.at[q], (x_to + [twin])[k])

    def d_twin(q):
        p = at(q)
        return remote(D.at[:, p], D.at[:, p], ds.at[3, q], dr.at[q], twin)

    def d_local(q):
        p = at(q)
        return pltpu.make_async_copy(G.at[(zl % 4) // 2, zl % 2, :, p], D.at[:, p], dr.at[q])

    for s in range(NS):
        for down in range(2):
            cross(s, down).wait_recv()
        for j in range(2):
            both = precv[0, s, j].astype(jnp.float32) + precv[1, s, j].astype(jnp.float32)
            G[s, j, y, (zl + 4) % NZL] = both.astype(jnp.bfloat16)
        for k in range(4):
            z_own(s, k).start()

    def do_z(q):
        for s in range(NS):
            @pl.when(q > 0)
            def _():
                remote(shard(s, q, y), shard(s, q, y), zf.at[s, q], zr.at[s, q], at_z(1)).wait_recv()

            @pl.when(goes_up(q))
            def _():
                z_up(s, q).start()

            @pl.when(goes_down(q))
            def _():
                z_down(s, q).start()

            for k in range(2):
                y_copy(s, k, q).start()

    def do_f(q):
        for s in range(NS):
            for k in range(2):
                y_copy(s, k, q).wait_recv()
            f_copy(s, q).start()

    def do_d0(q):
        for s in range(NS):
            f_copy(s, q).wait_recv()

        @pl.when(origin)
        def _():
            for k in (2, 0, 1, 3):
                d_copy(k, q).start()
            d_local(q).start()

    def do_d1(q):
        @pl.when(origin)
        def _():
            d_local(q).wait()

        @pl.when(relay)
        def _():
            d_twin(q).wait_recv()
            d_twin(q).start()

    def do_d2(q):
        @pl.when(jnp.logical_not(mine))
        def _():
            d_twin(q).wait_recv()

    def do_mm(q):
        p = at(q)
        for b in range(4):
            LT[b * 128 : (b + 1) * 128, :] = jnp.transpose(G[b // 2, b % 2, :, p].reshape(256, 128))
        dv = D[:, p].reshape(256, 128).astype(jnp.float32)
        for k in range(8):
            w = wide[k, :, p].reshape(256, 128)
            BS[k // 2, :, (k % 2) * 128 : (k % 2 + 1) * 128] = (w * dv).astype(jnp.bfloat16)
        for n in range(4):
            got = jnp.dot(LT[...], BS[n], preferred_element_type=jnp.float32)
            out[2 * n] += got[:, :128]
            out[2 * n + 1] += got[:, 128:]

    def during(t, lag, count, do):
        @pl.when(jnp.logical_and(t >= lag, t < lag + count))
        def _():
            do(t - lag)

    @pl.loop(0, LAGS[-1] + 8)
    def _(t):
        during(t, 0, 8, do_z)
        during(t, LAGS[0], 8, do_f)
        during(t, LAGS[1], 8, do_d0)
        during(t, LAGS[2], 8, do_d1)
        during(t, LAGS[3], 8, do_d2)
        during(t, LAGS[4], 8, do_mm)

    for s in range(NS):
        for down in range(2):
            cross(s, down).wait_send()
        for k in range(4):
            z_own(s, k).wait_send()

    @pl.loop(0, 8)
    def _(q):
        for s in range(NS):
            @pl.when(jnp.logical_or(goes_up(q), goes_down(q)))
            def _():
                z_up(s, q).wait_send()

            for k in range(2):
                y_copy(s, k, q).wait_send()
            f_copy(s, q).wait_send()

        @pl.when(origin)
        def _():
            for k in range(4):
                d_copy(k, q).wait_send()

        @pl.when(relay)
        def _():
            d_twin(q).wait_send()


def per_device(eigvecs, boundary, block_sizes, target_of_channel, poles, energies):
    rows = boundary.shape[0]
    bf, f32, dma = jnp.bfloat16, jnp.float32, pltpu.SemaphoreType.DMA
    given = (eigvecs, boundary, block_sizes, target_of_channel.reshape(4, 128), poles.reshape(16, 128), energies)
    return pl.pallas_call(
        kernel,
        out_shape=jax.ShapeDtypeStruct((8, 512, 128), f32),
        in_specs=[pl.BlockSpec(memory_space=pl.ANY)] * 6,
        out_specs=pl.BlockSpec(memory_space=pltpu.VMEM),
        scratch_shapes=[
            pltpu.SMEM((16,), jnp.int32),
            pltpu.VMEM((4, 128), jnp.int32),
            pltpu.VMEM((16, 128), f32),
            pltpu.SMEM((8,), f32),
            dma((4,)),
            pltpu.VMEM((64, rows), bf),
            pltpu.VMEM((rows, 512), bf),
            pltpu.VMEM((NS, 2, 64, 128), bf),
            pltpu.VMEM((2, NS, 2, 64, 128), bf),
            pltpu.VMEM((2, 2, NY, NZL, 64, 128), bf),
            pltpu.VMEM((NY, NZL, 64, 128), bf),
            pltpu.VMEM((8, 16, 128), f32),
            pltpu.VMEM((16, 128, 8), f32),
            pltpu.VMEM((8, NY, NZL, 64, 128), f32),
            pltpu.VMEM((512, 256), bf),
            pltpu.VMEM((4, 256, 256), bf),
            dma, dma((5,)), dma((NS, 2)), dma((NS, 2)),
            dma((NS, 4)), dma((NS, 8)), dma((NS, 8)),
            dma((NS, 2, 8)), dma((NS, 2, 8)),
            dma((NS, 8)), dma((NS, 8)),
            dma((4, 8)), dma((8,)),
        ],
        compiler_params=pltpu.CompilerParams(
            collective_id=0, has_side_effects=True, vmem_limit_bytes=42 * 2**20
        ),
        cost_estimate=pl.CostEstimate(flops=2_400_000_000, bytes_accessed=5_000_000, transcendentals=0),
    )(*(pltpu.with_memory_space_constraint(a, pltpu.HBM) for a in given))


def solution(mesh):
    placed = (P("eig", "basis"), P("basis", "chan"), P(), P("chan"), P(), P("basis"))
    return jax.shard_map(
        per_device, mesh=mesh, in_specs=placed, out_specs=P("basis", "chan", "eig"), check_vma=False
    )
```

```python
import jax
import jax.numpy as jnp
from jax import lax
from jax.experimental import pallas as pl
from jax.experimental.pallas import tpu as pltpu
from jax.sharding import PartitionSpec as P

MESH = pl.DeviceIdType.MESH
NY, NZL, NX, NZ = 4, 8, 4, 16
NS = 2
LAGS = (3, 5, 8, 9, 9)


def remote(src, dst, send, recv, where):
    return pltpu.make_async_remote_copy(
        src_ref=src, dst_ref=dst, send_sem=send, recv_sem=recv, device_id=where, device_id_type=MESH
    )


def kernel(
    eig_hbm, bnd_hbm, sizes_hbm, tgt_hbm, poles_hbm, energies_hbm, out,
    sizes, tgt, poles, energies, small_sem, eig, bnd, psend, precv, G, D, wrow, wcol, wide, LT, BS,
    eig_sem, bnd_sem, xs, xr, zs, zf, zr, ys, yr, fs, fr, ds, dr,
):
    h, e, c = lax.axis_index("basis"), lax.axis_index("eig"), lax.axis_index("chan")
    y, zl = e // NZL, e % NZL
    x, core = c // 2, c % 2
    z = h * NZL + zl
    rows = bnd.shape[0]

    def at_z(far):
        zz = (z + far + NZ) % NZ
        return (zz // NZL, y * NZL + zz % NZL, c)

    y_to = [(h, ((y + k) % NY) * NZL + zl, c) for k in (1, 3)]
    x_to = [(h, e, ((x + k) % NX) * 2 + core) for k in (1, 3, 2)]
    twin = (h, e, x * 2 + (1 - core))
    partners = [at_z(k) for k in (4, -4, 1, -1, 2, -2)] + y_to + x_to + [twin]

    barrier = pltpu.get_barrier_semaphore()
    for who in partners:
        pl.semaphore_signal(barrier, inc=1, device_id=who, device_id_type=MESH)

    small = [
        pltpu.make_async_copy(src, dst, small_sem.at[i])
        for i, (src, dst) in enumerate(
            ((sizes_hbm, sizes), (tgt_hbm, tgt), (poles_hbm, poles), (energies_hbm, energies))
        )
    ]
    eig_copy = pltpu.make_async_copy(eig_hbm, eig, eig_sem)

    step = rows // 5

    def bnd_copy(i):
        part = pl.ds(i * step, step)
        return pltpu.make_async_copy(bnd_hbm.at[part], bnd.at[part], bnd_sem.at[i])

    for copy in small:
        copy.start()
    eig_copy.start()
    for i in range(5):
        bnd_copy(i).start()
    for copy in small:
        copy.wait()

    def cross(s, down):
        return remote(psend.at[s], precv.at[down, s], xs.at[s, down], xr.at[s, down], at_z(4 - 8 * down))

    t = jnp.concatenate([tgt[b : b + 1, :] for b in range(4)], axis=1)
    lo = jnp.zeros((1, 512), jnp.int32)
    hi = jnp.zeros((1, 512), jnp.int32)
    for k in range(16):
        lo = lo + jnp.where(t > k, sizes[k], 0)
        hi = hi + jnp.where(t >= k, sizes[k], 0)
    lo = lo - h * rows
    hi = hi - h * rows
    eig_copy.wait()
    total = jnp.zeros((64, 512), jnp.float32)
    for i in range(5):
        bnd_copy(i).wait()
        row = lax.broadcasted_iota(jnp.int32, (step, 512), 0) + i * step
        keep = jnp.logical_and(row >= lo, row < hi)
        vals = bnd[i * step : (i + 1) * step, :].astype(jnp.float32)
        masked = jnp.where(keep, vals, 0.0).astype(jnp.bfloat16)
        total = total + jnp.dot(
            eig[:, i * step : (i + 1) * step], masked, preferred_element_type=jnp.float32
        )
    for b in range(4):
        psend[b // 2, b % 2] = total[:, b * 128 : (b + 1) * 128].astype(jnp.bfloat16)
    pl.semaphore_wait(barrier, len(partners))
    for s in range(NS):
        for down in range(2):
            cross(s, down).start()

    for k in range(8):
        wrow[k] = (wrow.shape[1] * 128) ** -0.5 / (poles[...] - energies[k])
    for i in range(16):
        wcol[i] = jnp.transpose(wrow[:, i, :])

    @pl.loop(0, 16)
    def _(i):
        for k in range(8):
            across = jnp.broadcast_to(wcol[i, :, k : k + 1], (128, 128))
            wide[k, i // 4, pl.ds((i % 4) * 2, 2)] = across.reshape(2, 64, 128)

    @pl.loop(0, 8)
    def _(k):
        out[k] = jnp.zeros(out.shape[1:], jnp.float32)

    def at(q):
        return (zl + ((q + 1) // 2) * (1 - 2 * (q % 2)) + 12) % NZL

    def shard(s, q, yy):
        return G.at[s, :, yy, at(q)]

    def z_own(s, k):
        far, q = ((1, 1), (-1, 2), (2, 3), (-2, 4))[k]
        return remote(shard(s, 0, y), shard(s, 0, y), zs.at[s, k], zr.at[s, q], at_z(far))

    def z_up(s, q):
        return remote(shard(s, q, y), shard(s, q, y), zf.at[s, q], zr.at[s, q + 4], at_z(2))

    def z_down(s, q):
        return remote(shard(s, q, y), shard(s, q, y), zf.at[s, q], zr.at[s, q + 4 - q // 4], at_z(-2))

    def goes_up(q):
        return jnp.logical_and(q % 2 == 1, q + core < 4)

    def goes_down(q):
        return jnp.logical_and(jnp.logical_and(q % 2 == 0, q > 0), q < 4 + core)

    def y_copy(s, k, q):
        return remote(shard(s, q, y), shard(s, q, y), ys.at[s, k, q], yr.at[s, k, q], y_to[k])

    def f_copy(s, q):
        yy = (y + 3 - 2 * core) % NY
        to = (h, ((y + 1 + 2 * core) % NY) * NZL + zl, c)
        return remote(shard(s, q, yy), shard(s, q, yy), fs.at[s, q], fr.at[s, q], to)

    kap = zl // 4
    r = (x - y + NX) % NX
    mine = core == kap
    origin = jnp.logical_and(mine, r == 0)
    relay = jnp.logical_and(mine, r != 0)

    def d_copy(k, q):
        p = at(q)
        return remote(G.at[(zl % 4) // 2, zl % 2, :, p], D.at[:, p], ds.at[k, q], dr.at[q], (x_to + [twin])[k])

    def d_twin(q):
        p = at(q)
        return remote(D.at[:, p], D.at[:, p], ds.at[3, q], dr.at[q], twin)

    def d_local(q):
        p = at(q)
        return pltpu.make_async_copy(G.at[(zl % 4) // 2, zl % 2, :, p], D.at[:, p], dr.at[q])

    for s in range(NS):
        for down in range(2):
            cross(s, down).wait_recv()
        for j in range(2):
            both = precv[0, s, j].astype(jnp.float32) + precv[1, s, j].astype(jnp.float32)
            G[s, j, y, (zl + 4) % NZL] = both.astype(jnp.bfloat16)
        for k in range(2):
            z_own(s, k).start()
            y_copy(s, k, 0).start()
        for k in range(2, 4):
            z_own(s, k).start()

    def do_z(q):
        for s in range(NS):
            remote(shard(s, q, y), shard(s, q, y), zf.at[s, q], zr.at[s, q], at_z(1)).wait_recv()

            for k in range(2):
                y_copy(s, k, q).start()

            @pl.when(goes_up(q))
            def _():
                z_up(s, q).start()

            @pl.when(goes_down(q))
            def _():
                z_down(s, q).start()

    def do_f(q):
        for s in range(NS):
            for k in range(2):
                y_copy(s, k, q).wait_recv()
            f_copy(s, q).start()

    def do_d0(q):
        for s in range(NS):
            f_copy(s, q).wait_recv()

        @pl.when(origin)
        def _():
            for k in (2, 0, 1, 3):
                d_copy(k, q).start()
            d_local(q).start()

    def do_d1(q):
        @pl.when(origin)
        def _():
            d_local(q).wait()

        @pl.when(relay)
        def _():
            d_twin(q).wait_recv()
            d_twin(q).start()

    def do_d2(q):
        @pl.when(jnp.logical_not(mine))
        def _():
            d_twin(q).wait_recv()

    def do_mm(q):
        p = at(q)
        for b in range(4):
            LT[b * 128 : (b + 1) * 128, :] = jnp.transpose(G[b // 2, b % 2, :, p].reshape(256, 128))
        dv = D[:, p].reshape(256, 128).astype(jnp.float32)
        for k in range(8):
            w = wide[k, :, p].reshape(256, 128)
            BS[k // 2, :, (k % 2) * 128 : (k % 2 + 1) * 128] = (w * dv).astype(jnp.bfloat16)
        for n in range(4):
            got = jnp.dot(LT[...], BS[n], preferred_element_type=jnp.float32)
            out[2 * n] += got[:, :128]
            out[2 * n + 1] += got[:, 128:]

    def during(t, lag, count, do):
        @pl.when(jnp.logical_and(t >= lag, t < lag + count))
        def _():
            do(t - lag)

    @pl.loop(0, LAGS[-1] + 8)
    def _(t):
        @pl.when(jnp.logical_and(t >= 1, t < 8))
        def _():
            do_z(t)

        during(t, LAGS[0], 8, do_f)
        during(t, LAGS[1], 8, do_d0)
        during(t, LAGS[2], 8, do_d1)
        during(t, LAGS[3], 8, do_d2)
        during(t, LAGS[4], 8, do_mm)

    for s in range(NS):
        for down in range(2):
            cross(s, down).wait_send()
        for k in range(4):
            z_own(s, k).wait_send()

    @pl.loop(0, 8)
    def _(q):
        for s in range(NS):
            @pl.when(jnp.logical_or(goes_up(q), goes_down(q)))
            def _():
                z_up(s, q).wait_send()

            for k in range(2):
                y_copy(s, k, q).wait_send()
            f_copy(s, q).wait_send()

        @pl.when(origin)
        def _():
            for k in range(4):
                d_copy(k, q).wait_send()

        @pl.when(relay)
        def _():
            d_twin(q).wait_send()


def per_device(eigvecs, boundary, block_sizes, target_of_channel, poles, energies):
    rows = boundary.shape[0]
    bf, f32, dma = jnp.bfloat16, jnp.float32, pltpu.SemaphoreType.DMA
    given = (eigvecs, boundary, block_sizes, target_of_channel.reshape(4, 128), poles.reshape(16, 128), energies)
    return pl.pallas_call(
        kernel,
        out_shape=jax.ShapeDtypeStruct((8, 512, 128), f32),
        in_specs=[pl.BlockSpec(memory_space=pl.ANY)] * 6,
        out_specs=pl.BlockSpec(memory_space=pltpu.VMEM),
        scratch_shapes=[
            pltpu.SMEM((16,), jnp.int32),
            pltpu.VMEM((4, 128), jnp.int32),
            pltpu.VMEM((16, 128), f32),
            pltpu.SMEM((8,), f32),
            dma((4,)),
            pltpu.VMEM((64, rows), bf),
            pltpu.VMEM((rows, 512), bf),
            pltpu.VMEM((NS, 2, 64, 128), bf),
            pltpu.VMEM((2, NS, 2, 64, 128), bf),
            pltpu.VMEM((2, 2, NY, NZL, 64, 128), bf),
            pltpu.VMEM((NY, NZL, 64, 128), bf),
            pltpu.VMEM((8, 16, 128), f32),
            pltpu.VMEM((16, 128, 8), f32),
            pltpu.VMEM((8, NY, NZL, 64, 128), f32),
            pltpu.VMEM((512, 256), bf),
            pltpu.VMEM((4, 256, 256), bf),
            dma, dma((5,)), dma((NS, 2)), dma((NS, 2)),
            dma((NS, 4)), dma((NS, 8)), dma((NS, 8)),
            dma((NS, 2, 8)), dma((NS, 2, 8)),
            dma((NS, 8)), dma((NS, 8)),
            dma((4, 8)), dma((8,)),
        ],
        compiler_params=pltpu.CompilerParams(
            collective_id=0, has_side_effects=True, vmem_limit_bytes=42 * 2**20
        ),
        cost_estimate=pl.CostEstimate(flops=2_400_000_000, bytes_accessed=5_000_000, transcendentals=0),
    )(*(pltpu.with_memory_space_constraint(a, pltpu.HBM) for a in given))


def solution(mesh):
    placed = (P("eig", "basis"), P("basis", "chan"), P(), P("chan"), P(), P("basis"))
    return jax.shard_map(
        per_device, mesh=mesh, in_specs=placed, out_specs=P("basis", "chan", "eig"), check_vma=False
    )
```

```python
import jax
import jax.numpy as jnp
from jax import lax
from jax.experimental import pallas as pl
from jax.experimental.pallas import tpu as pltpu
from jax.sharding import PartitionSpec as P

MESH = pl.DeviceIdType.MESH
NY, NZL, NX, NZ = 4, 8, 4, 16
NS = 2
LAGS = (3, 5, 8, 9, 9)


def remote(src, dst, send, recv, where):
    return pltpu.make_async_remote_copy(
        src_ref=src, dst_ref=dst, send_sem=send, recv_sem=recv, device_id=where, device_id_type=MESH
    )


def kernel(
    eig_hbm, bnd_hbm, sizes_hbm, tgt_hbm, poles_hbm, energies_hbm, out,
    sizes, tgt, poles, energies, small_sem, eig, bnd, psend, precv, G, D, wrow, wcol, wide, LT, BS,
    eig_sem, bnd_sem, xs, xr, zs, zf, zr, ys, yr, fs, fr, ds, dr,
):
    h, e, c = lax.axis_index("basis"), lax.axis_index("eig"), lax.axis_index("chan")
    y, zl = e // NZL, e % NZL
    x, core = c // 2, c % 2
    z = h * NZL + zl
    rows = bnd.shape[0]

    def at_z(far):
        zz = (z + far + NZ) % NZ
        return (zz // NZL, y * NZL + zz % NZL, c)

    y_to = [(h, ((y + k) % NY) * NZL + zl, c) for k in (1, 3)]
    x_to = [(h, e, ((x + k) % NX) * 2 + core) for k in (1, 3, 2)]
    twin = (h, e, x * 2 + (1 - core))
    partners = [at_z(k) for k in (4, -4, 1, -1, 2, -2)] + y_to + x_to + [twin]

    barrier = pltpu.get_barrier_semaphore()
    for who in partners:
        pl.semaphore_signal(barrier, inc=1, device_id=who, device_id_type=MESH)

    small = [
        pltpu.make_async_copy(src, dst, small_sem.at[i])
        for i, (src, dst) in enumerate(
            ((sizes_hbm, sizes), (tgt_hbm, tgt), (poles_hbm, poles), (energies_hbm, energies))
        )
    ]
    eig_copy = pltpu.make_async_copy(eig_hbm, eig, eig_sem)

    step = rows // 5

    def bnd_copy(i):
        part = pl.ds(i * step, step)
        return pltpu.make_async_copy(bnd_hbm.at[part], bnd.at[part], bnd_sem.at[i])

    for copy in small:
        copy.start()
    eig_copy.start()
    for i in range(5):
        bnd_copy(i).start()
    for copy in small:
        copy.wait()

    def cross(s, down):
        return remote(psend.at[s], precv.at[down, s], xs.at[s, down], xr.at[s, down], at_z(4 - 8 * down))

    t = jnp.concatenate([tgt[b : b + 1, :] for b in range(4)], axis=1)
    lo = jnp.zeros((1, 512), jnp.int32)
    hi = jnp.zeros((1, 512), jnp.int32)
    for k in range(16):
        lo = lo + jnp.where(t > k, sizes[k], 0)
        hi = hi + jnp.where(t >= k, sizes[k], 0)
    lo = lo - h * rows
    hi = hi - h * rows
    eig_copy.wait()
    total = jnp.zeros((64, 512), jnp.float32)
    for i in range(5):
        bnd_copy(i).wait()
        row = lax.broadcasted_iota(jnp.int32, (step, 512), 0) + i * step
        keep = jnp.logical_and(row >= lo, row < hi)
        vals = bnd[i * step : (i + 1) * step, :].astype(jnp.float32)
        masked = jnp.where(keep, vals, 0.0).astype(jnp.bfloat16)
        total = total + jnp.dot(
            eig[:, i * step : (i + 1) * step], masked, preferred_element_type=jnp.float32
        )
    for b in range(4):
        psend[b // 2, b % 2] = total[:, b * 128 : (b + 1) * 128].astype(jnp.bfloat16)
    pl.semaphore_wait(barrier, len(partners))
    for s in range(NS):
        for down in range(2):
            cross(s, down).start()

    for k in range(8):
        wrow[k] = (wrow.shape[1] * 128) ** -0.5 / (poles[...] - energies[k])
    for i in range(16):
        wcol[i] = jnp.transpose(wrow[:, i, :])

    @pl.loop(0, 16)
    def _(i):
        for k in range(8):
            across = jnp.broadcast_to(wcol[i, :, k : k + 1], (128, 128))
            wide[k, i // 4, pl.ds((i % 4) * 2, 2)] = across.reshape(2, 64, 128)

    @pl.loop(0, 8)
    def _(k):
        out[k] = jnp.zeros(out.shape[1:], jnp.float32)

    def at(q):
        return (zl + ((q + 1) // 2) * (1 - 2 * (q % 2)) + 12) % NZL

    def shard(s, q, yy):
        return G.at[s, :, yy, at(q)]

    def z_own(s, k):
        far, q = ((1, 1), (-1, 2), (2, 3), (-2, 4))[k]
        return remote(shard(s, 0, y), shard(s, 0, y), zs.at[s, k], zr.at[s, q], at_z(far))

    def z_up(s, q):
        return remote(shard(s, q, y), shard(s, q, y), zf.at[s, q], zr.at[s, q + 4], at_z(2))

    def z_down(s, q):
        return remote(shard(s, q, y), shard(s, q, y), zf.at[s, q], zr.at[s, q + 4 - q // 4], at_z(-2))

    def goes_up(q):
        return jnp.logical_and(q % 2 == 1, q + core < 4)

    def goes_down(q):
        return jnp.logical_and(jnp.logical_and(q % 2 == 0, q > 0), q < 4 + core)

    def y_copy(s, k, q):
        return remote(shard(s, q, y), shard(s, q, y), ys.at[s, k, q], yr.at[s, k, q], y_to[k])

    def f_copy(s, q):
        yy = (y + 3 - 2 * core) % NY
        to = (h, ((y + 1 + 2 * core) % NY) * NZL + zl, c)
        return remote(shard(s, q, yy), shard(s, q, yy), fs.at[s, q], fr.at[s, q], to)

    kap = zl // 4
    first = (zl % 4) // 2
    order = (first, 1 - first)
    r = (x - y + NX) % NX
    mine = core == kap
    origin = jnp.logical_and(mine, r == 0)
    relay = jnp.logical_and(mine, r != 0)

    def d_copy(k, q):
        p = at(q)
        return remote(G.at[(zl % 4) // 2, zl % 2, :, p], D.at[:, p], ds.at[k, q], dr.at[q], (x_to + [twin])[k])

    def d_twin(q):
        p = at(q)
        return remote(D.at[:, p], D.at[:, p], ds.at[3, q], dr.at[q], twin)

    def d_local(q):
        p = at(q)
        return pltpu.make_async_copy(G.at[(zl % 4) // 2, zl % 2, :, p], D.at[:, p], dr.at[q])

    for s in range(NS):
        for down in range(2):
            cross(s, down).wait_recv()
        for j in range(2):
            both = precv[0, s, j].astype(jnp.float32) + precv[1, s, j].astype(jnp.float32)
            G[s, j, y, (zl + 4) % NZL] = both.astype(jnp.bfloat16)
        for k in range(2):
            z_own(s, k).start()
            y_copy(s, k, 0).start()
        for k in range(2, 4):
            z_own(s, k).start()

    def do_z(q):
        for s in order:
            remote(shard(s, q, y), shard(s, q, y), zf.at[s, q], zr.at[s, q], at_z(1)).wait_recv()

            for k in range(2):
                y_copy(s, k, q).start()

            @pl.when(goes_up(q))
            def _():
                z_up(s, q).start()

            @pl.when(goes_down(q))
            def _():
                z_down(s, q).start()

    def do_f(q):
        for s in order:
            for k in range(2):
                y_copy(s, k, q).wait_recv()
            f_copy(s, q).start()

    def do_d0(q):
        f_copy(first, q).wait_recv()

        @pl.when(origin)
        def _():
            for k in (2, 0, 1, 3):
                d_copy(k, q).start()
            d_local(q).start()

    def do_d1(q):
        f_copy(1 - first, q).wait_recv()

        @pl.when(origin)
        def _():
            d_local(q).wait()

        @pl.when(relay)
        def _():
            d_twin(q).wait_recv()
            d_twin(q).start()

    def do_d2(q):
        @pl.when(jnp.logical_not(mine))
        def _():
            d_twin(q).wait_recv()

    def do_mm(q):
        p = at(q)
        for b in range(4):
            LT[b * 128 : (b + 1) * 128, :] = jnp.transpose(G[b // 2, b % 2, :, p].reshape(256, 128))
        dv = D[:, p].reshape(256, 128).astype(jnp.float32)
        for k in range(8):
            w = wide[k, :, p].reshape(256, 128)
            BS[k // 2, :, (k % 2) * 128 : (k % 2 + 1) * 128] = (w * dv).astype(jnp.bfloat16)
        for n in range(4):
            got = jnp.dot(LT[...], BS[n], preferred_element_type=jnp.float32)
            out[2 * n] += got[:, :128]
            out[2 * n + 1] += got[:, 128:]

    def during(t, lag, count, do):
        @pl.when(jnp.logical_and(t >= lag, t < lag + count))
        def _():
            do(t - lag)

    @pl.loop(0, LAGS[-1] + 8)
    def _(t):
        @pl.when(jnp.logical_and(t >= 1, t < 8))
        def _():
            do_z(t)

        during(t, LAGS[0], 8, do_f)
        during(t, LAGS[1], 8, do_d0)
        during(t, LAGS[2], 8, do_d1)
        during(t, LAGS[3], 8, do_d2)
        during(t, LAGS[4], 8, do_mm)

    for s in range(NS):
        for down in range(2):
            cross(s, down).wait_send()
        for k in range(4):
            z_own(s, k).wait_send()

    @pl.loop(0, 8)
    def _(q):
        for s in range(NS):
            @pl.when(jnp.logical_or(goes_up(q), goes_down(q)))
            def _():
                z_up(s, q).wait_send()

            for k in range(2):
                y_copy(s, k, q).wait_send()
            f_copy(s, q).wait_send()

        @pl.when(origin)
        def _():
            for k in range(4):
                d_copy(k, q).wait_send()

        @pl.when(relay)
        def _():
            d_twin(q).wait_send()


def per_device(eigvecs, boundary, block_sizes, target_of_channel, poles, energies):
    rows = boundary.shape[0]
    bf, f32, dma = jnp.bfloat16, jnp.float32, pltpu.SemaphoreType.DMA
    given = (eigvecs, boundary, block_sizes, target_of_channel.reshape(4, 128), poles.reshape(16, 128), energies)
    return pl.pallas_call(
        kernel,
        out_shape=jax.ShapeDtypeStruct((8, 512, 128), f32),
        in_specs=[pl.BlockSpec(memory_space=pl.ANY)] * 6,
        out_specs=pl.BlockSpec(memory_space=pltpu.VMEM),
        scratch_shapes=[
            pltpu.SMEM((16,), jnp.int32),
            pltpu.VMEM((4, 128), jnp.int32),
            pltpu.VMEM((16, 128), f32),
            pltpu.SMEM((8,), f32),
            dma((4,)),
            pltpu.VMEM((64, rows), bf),
            pltpu.VMEM((rows, 512), bf),
            pltpu.VMEM((NS, 2, 64, 128), bf),
            pltpu.VMEM((2, NS, 2, 64, 128), bf),
            pltpu.VMEM((2, 2, NY, NZL, 64, 128), bf),
            pltpu.VMEM((NY, NZL, 64, 128), bf),
            pltpu.VMEM((8, 16, 128), f32),
            pltpu.VMEM((16, 128, 8), f32),
            pltpu.VMEM((8, NY, NZL, 64, 128), f32),
            pltpu.VMEM((512, 256), bf),
            pltpu.VMEM((4, 256, 256), bf),
            dma, dma((5,)), dma((NS, 2)), dma((NS, 2)),
            dma((NS, 4)), dma((NS, 8)), dma((NS, 8)),
            dma((NS, 2, 8)), dma((NS, 2, 8)),
            dma((NS, 8)), dma((NS, 8)),
            dma((4, 8)), dma((8,)),
        ],
        compiler_params=pltpu.CompilerParams(
            collective_id=0, has_side_effects=True, vmem_limit_bytes=42 * 2**20
        ),
        cost_estimate=pl.CostEstimate(flops=2_400_000_000, bytes_accessed=5_000_000, transcendentals=0),
    )(*(pltpu.with_memory_space_constraint(a, pltpu.HBM) for a in given))


def solution(mesh):
    placed = (P("eig", "basis"), P("basis", "chan"), P(), P("chan"), P(), P("basis"))
    return jax.shard_map(
        per_device, mesh=mesh, in_specs=placed, out_specs=P("basis", "chan", "eig"), check_vma=False
    )
```

```python
import jax
import jax.numpy as jnp
from jax import lax
from jax.experimental import pallas as pl
from jax.experimental.pallas import tpu as pltpu
from jax.sharding import PartitionSpec as P

MESH = pl.DeviceIdType.MESH
NY, NZL, NX, NZ = 4, 8, 4, 16
NS = 2
LAGS = (3, 6, 9, 10, 10)


def remote(src, dst, send, recv, where):
    return pltpu.make_async_remote_copy(
        src_ref=src, dst_ref=dst, send_sem=send, recv_sem=recv, device_id=where, device_id_type=MESH
    )


def kernel(
    eig_hbm, bnd_hbm, sizes_hbm, tgt_hbm, poles_hbm, energies_hbm, out,
    sizes, tgt, poles, energies, small_sem, eig, bnd, psend, precv, G, D, wrow, wcol, wide, LT, BS,
    eig_sem, bnd_sem, xs, xr, zs, zf, zr, ys, yr, fs, fr, ds, dr,
):
    h, e, c = lax.axis_index("basis"), lax.axis_index("eig"), lax.axis_index("chan")
    y, zl = e // NZL, e % NZL
    x, core = c // 2, c % 2
    z = h * NZL + zl
    rows = bnd.shape[0]

    def at_z(far):
        zz = (z + far + NZ) % NZ
        return (zz // NZL, y * NZL + zz % NZL, c)

    y_to = [(h, ((y + k) % NY) * NZL + zl, c) for k in (1, 3)]
    x_to = [(h, e, ((x + k) % NX) * 2 + core) for k in (1, 3, 2)]
    twin = (h, e, x * 2 + (1 - core))
    partners = [at_z(k) for k in (4, -4, 1, -1, 2, -2)] + y_to + x_to + [twin]

    barrier = pltpu.get_barrier_semaphore()
    for who in partners:
        pl.semaphore_signal(barrier, inc=1, device_id=who, device_id_type=MESH)

    small = [
        pltpu.make_async_copy(src, dst, small_sem.at[i])
        for i, (src, dst) in enumerate(
            ((sizes_hbm, sizes), (tgt_hbm, tgt), (poles_hbm, poles), (energies_hbm, energies))
        )
    ]
    eig_copy = pltpu.make_async_copy(eig_hbm, eig, eig_sem)

    step = rows // 5

    def bnd_copy(i):
        part = pl.ds(i * step, step)
        return pltpu.make_async_copy(bnd_hbm.at[part], bnd.at[part], bnd_sem.at[i])

    for copy in small:
        copy.start()
    eig_copy.start()
    for i in range(5):
        bnd_copy(i).start()
    for copy in small:
        copy.wait()

    def cross(s, down):
        return remote(psend.at[s], precv.at[down, s], xs.at[s, down], xr.at[s, down], at_z(4 - 8 * down))

    t = jnp.concatenate([tgt[b : b + 1, :] for b in range(4)], axis=1)
    lo = jnp.zeros((1, 512), jnp.int32)
    hi = jnp.zeros((1, 512), jnp.int32)
    for k in range(16):
        lo = lo + jnp.where(t > k, sizes[k], 0)
        hi = hi + jnp.where(t >= k, sizes[k], 0)
    lo = lo - h * rows
    hi = hi - h * rows
    eig_copy.wait()
    total = jnp.zeros((64, 512), jnp.float32)
    for i in range(5):
        bnd_copy(i).wait()
        row = lax.broadcasted_iota(jnp.int32, (step, 512), 0) + i * step
        keep = jnp.logical_and(row >= lo, row < hi)
        vals = bnd[i * step : (i + 1) * step, :].astype(jnp.float32)
        masked = jnp.where(keep, vals, 0.0).astype(jnp.bfloat16)
        total = total + jnp.dot(
            eig[:, i * step : (i + 1) * step], masked, preferred_element_type=jnp.float32
        )
    for b in range(4):
        psend[b // 2, b % 2] = total[:, b * 128 : (b + 1) * 128].astype(jnp.bfloat16)
    pl.semaphore_wait(barrier, len(partners))
    for s in range(NS):
        for down in range(2):
            cross(s, down).start()

    for k in range(8):
        wrow[k] = (wrow.shape[1] * 128) ** -0.5 / (poles[...] - energies[k])
    for i in range(16):
        wcol[i] = jnp.transpose(wrow[:, i, :])

    @pl.loop(0, 16)
    def _(i):
        for k in range(8):
            across = jnp.broadcast_to(wcol[i, :, k : k + 1], (128, 128))
            wide[k, i // 4, pl.ds((i % 4) * 2, 2)] = across.reshape(2, 64, 128)

    @pl.loop(0, 8)
    def _(k):
        out[k] = jnp.zeros(out.shape[1:], jnp.float32)

    def at(q):
        return (zl + ((q + 1) // 2) * (1 - 2 * (q % 2)) + 12) % NZL

    def shard(s, q, yy):
        return G.at[s, :, yy, at(q)]

    def z_own(s, k):
        far, q = ((1, 1), (-1, 2), (2, 3), (-2, 4))[k]
        return remote(shard(s, 0, y), shard(s, 0, y), zs.at[s, k], zr.at[s, q], at_z(far))

    def z_up(s, q):
        return remote(shard(s, q, y), shard(s, q, y), zf.at[s, q], zr.at[s, q + 4], at_z(2))

    def z_down(s, q):
        return remote(shard(s, q, y), shard(s, q, y), zf.at[s, q], zr.at[s, q + 4 - q // 4], at_z(-2))

    def goes_up(q):
        return jnp.logical_and(q % 2 == 1, q + core < 4)

    def goes_down(q):
        return jnp.logical_and(jnp.logical_and(q % 2 == 0, q > 0), q < 4 + core)

    def y_copy(s, k, q):
        return remote(shard(s, q, y), shard(s, q, y), ys.at[s, k, q], yr.at[s, k, q], y_to[k])

    def f_copy(s, q):
        yy = (y + 3 - 2 * core) % NY
        to = (h, ((y + 1 + 2 * core) % NY) * NZL + zl, c)
        return remote(shard(s, q, yy), shard(s, q, yy), fs.at[s, q], fr.at[s, q], to)

    kap = zl // 4
    r = (x - y + NX) % NX
    mine = core == kap
    origin = jnp.logical_and(mine, r == 0)
    relay = jnp.logical_and(mine, r != 0)

    def d_copy(k, q):
        p = at(q)
        return remote(G.at[(zl % 4) // 2, zl % 2, :, p], D.at[:, p], ds.at[k, q], dr.at[q], (x_to + [twin])[k])

    def d_twin(q):
        p = at(q)
        return remote(D.at[:, p], D.at[:, p], ds.at[3, q], dr.at[q], twin)

    def d_local(q):
        p = at(q)
        return pltpu.make_async_copy(G.at[(zl % 4) // 2, zl % 2, :, p], D.at[:, p], dr.at[q])

    for s in range(NS):
        for down in range(2):
            cross(s, down).wait_recv()
        for j in range(2):
            both = precv[0, s, j].astype(jnp.float32) + precv[1, s, j].astype(jnp.float32)
            G[s, j, y, (zl + 4) % NZL] = both.astype(jnp.bfloat16)
        for k in range(2):
            z_own(s, k).start()
            y_copy(s, k, 0).start()
        for k in range(2, 4):
            z_own(s, k).start()

    def do_z(q):
        for s in range(NS):
            remote(shard(s, q, y), shard(s, q, y), zf.at[s, q], zr.at[s, q], at_z(1)).wait_recv()

            for k in range(2):
                y_copy(s, k, q).start()

            @pl.when(goes_up(q))
            def _():
                z_up(s, q).start()

            @pl.when(goes_down(q))
            def _():
                z_down(s, q).start()

    def do_f(q):
        for s in range(NS):
            for k in range(2):
                y_copy(s, k, q).wait_recv()
            f_copy(s, q).start()

    def do_d0(q):
        for s in range(NS):
            f_copy(s, q).wait_recv()

        @pl.when(origin)
        def _():
            for k in (2, 0, 1, 3):
                d_copy(k, q).start()
            d_local(q).start()

    def do_d1(q):
        @pl.when(origin)
        def _():
            d_local(q).wait()

        @pl.when(relay)
        def _():
            d_twin(q).wait_recv()
            d_twin(q).start()

    def do_d2(q):
        @pl.when(jnp.logical_not(mine))
        def _():
            d_twin(q).wait_recv()

    def do_mm(q):
        p = at(q)
        for b in range(4):
            LT[b * 128 : (b + 1) * 128, :] = jnp.transpose(G[b // 2, b % 2, :, p].reshape(256, 128))
        dv = D[:, p].reshape(256, 128).astype(jnp.float32)
        for k in range(8):
            w = wide[k, :, p].reshape(256, 128)
            BS[k // 2, :, (k % 2) * 128 : (k % 2 + 1) * 128] = (w * dv).astype(jnp.bfloat16)
        for n in range(4):
            got = jnp.dot(LT[...], BS[n], preferred_element_type=jnp.float32)
            out[2 * n] += got[:, :128]
            out[2 * n + 1] += got[:, 128:]

    def during(t, lag, count, do):
        @pl.when(jnp.logical_and(t >= lag, t < lag + count))
        def _():
            do(t - lag)

    @pl.loop(0, LAGS[-1] + 8)
    def _(t):
        @pl.when(jnp.logical_and(t >= 1, t < 8))
        def _():
            do_z(t)

        during(t, LAGS[0], 8, do_f)
        during(t, LAGS[1], 8, do_d0)
        during(t, LAGS[2], 8, do_d1)
        during(t, LAGS[3], 8, do_d2)
        during(t, LAGS[4], 8, do_mm)

    for s in range(NS):
        for down in range(2):
            cross(s, down).wait_send()
        for k in range(4):
            z_own(s, k).wait_send()

    @pl.loop(0, 8)
    def _(q):
        for s in range(NS):
            @pl.when(jnp.logical_or(goes_up(q), goes_down(q)))
            def _():
                z_up(s, q).wait_send()

            for k in range(2):
                y_copy(s, k, q).wait_send()
            f_copy(s, q).wait_send()

        @pl.when(origin)
        def _():
            for k in range(4):
                d_copy(k, q).wait_send()

        @pl.when(relay)
        def _():
            d_twin(q).wait_send()


def per_device(eigvecs, boundary, block_sizes, target_of_channel, poles, energies):
    rows = boundary.shape[0]
    bf, f32, dma = jnp.bfloat16, jnp.float32, pltpu.SemaphoreType.DMA
    given = (eigvecs, boundary, block_sizes, target_of_channel.reshape(4, 128), poles.reshape(16, 128), energies)
    return pl.pallas_call(
        kernel,
        out_shape=jax.ShapeDtypeStruct((8, 512, 128), f32),
        in_specs=[pl.BlockSpec(memory_space=pl.ANY)] * 6,
        out_specs=pl.BlockSpec(memory_space=pltpu.VMEM),
        scratch_shapes=[
            pltpu.SMEM((16,), jnp.int32),
            pltpu.VMEM((4, 128), jnp.int32),
            pltpu.VMEM((16, 128), f32),
            pltpu.SMEM((8,), f32),
            dma((4,)),
            pltpu.VMEM((64, rows), bf),
            pltpu.VMEM((rows, 512), bf),
            pltpu.VMEM((NS, 2, 64, 128), bf),
            pltpu.VMEM((2, NS, 2, 64, 128), bf),
            pltpu.VMEM((2, 2, NY, NZL, 64, 128), bf),
            pltpu.VMEM((NY, NZL, 64, 128), bf),
            pltpu.VMEM((8, 16, 128), f32),
            pltpu.VMEM((16, 128, 8), f32),
            pltpu.VMEM((8, NY, NZL, 64, 128), f32),
            pltpu.VMEM((512, 256), bf),
            pltpu.VMEM((4, 256, 256), bf),
            dma, dma((5,)), dma((NS, 2)), dma((NS, 2)),
            dma((NS, 4)), dma((NS, 8)), dma((NS, 8)),
            dma((NS, 2, 8)), dma((NS, 2, 8)),
            dma((NS, 8)), dma((NS, 8)),
            dma((4, 8)), dma((8,)),
        ],
        compiler_params=pltpu.CompilerParams(
            collective_id=0, has_side_effects=True, vmem_limit_bytes=42 * 2**20
        ),
        cost_estimate=pl.CostEstimate(flops=2_400_000_000, bytes_accessed=5_000_000, transcendentals=0),
    )(*(pltpu.with_memory_space_constraint(a, pltpu.HBM) for a in given))


def solution(mesh):
    placed = (P("eig", "basis"), P("basis", "chan"), P(), P("chan"), P(), P("basis"))
    return jax.shard_map(
        per_device, mesh=mesh, in_specs=placed, out_specs=P("basis", "chan", "eig"), check_vma=False
    )
```
